256 devices in a mesh: sec: 2 (over y_lo), tp: 8 (over y_hi, x), dp: 16 (over z, core).
Axes of the slice: x: 4, y: 4 (y_hi: 2, y_lo: 2; y = y_hi * 2 + y_lo), z: 8, core: 2. Of those that a mesh axis runs over, the one named last changes fastest.
Arguments:
- student_input: bfloat16 [2048, 4096], P('dp', ('sec', 'tp')), may hold values from -6 to 6
- teacher_hidden: bfloat16 [2048, 16384], P('dp', ('sec', 'tp')), may hold values from -10 to 10
- projector: bfloat16 [16384, 4096], P(('sec', 'tp'), 'dp'), may hold values from -0.0625 to 0.0625
- gate_weight: bfloat16 [7168, 4096], P(('sec', 'tp')), may hold values from -0.09375 to 0.09375
- up_weight: bfloat16 [7168, 4096], P(('sec', 'tp')), may hold values from -0.09375 to 0.09375
- down_weight: bfloat16 [7168, 4096], P(('sec', 'tp')), may hold values from -0.0625 to 0.0625
Outputs:
- distill_loss: float32 [], replicated
- grad_gate: float32 [7168, 4096], P(('sec', 'tp'), 'dp')
- grad_up: float32 [7168, 4096], P(('sec', 'tp'), 'dp')
- grad_down: float32 [7168, 4096], P(('sec', 'tp'), 'dp')
The draws below stay inside these ranges and needn't reach their ends.
All inputs are finite; a program needn't handle non-finite values.
Results may differ from the reference program's by a relative error of at most 0.0041.
Values may be sent and summed in bfloat16 or wider, within the bound.
No kernel may reach another device: no remote copies, remote signals or barrier semaphores. Data moves between devices by JAX's collectives and lax.ppermute only.
A program may use at most 128 MiB of HBM per device.

```python
import math
import jax
import jax.numpy as jnp
from jax import lax

D = 4096
TW = 16384
FW = 7168
TOKENS = 2048


def draw_teacher_hidden(key, part):
    key = jax.random.fold_in(key, 11)
    first_key, second_key = jax.random.split(key, 2)
    position = jnp.arange(TW, dtype=jnp.float32) / TW
    rough = jax.random.uniform(second_key, (TW,), jnp.float32, 0.7, 1.4)
    base = jnp.clip(jax.random.normal(first_key, (TOKENS, TW), jnp.float32), -4.0, 4.0)
    rising = jnp.exp(position * math.log(3.0)) / 1.7
    return (base * (rising * rough)[None, :]).astype(jnp.bfloat16)


def raised(result, key, source, target, blocks, factor):
    owner, partner = [(jnp.arange(result.shape[dim]) // (result.shape[dim] // blocks)).reshape([-1 if axis == dim else 1 for axis in range(result.ndim)]) for dim in (source, target)]
    chosen = jax.random.permutation(key, blocks)[partner]
    strong = (owner == chosen) | (owner == (partner + blocks // 2) % blocks)
    return jnp.where(strong, factor * result, result)


def shard_levels(key, extent, shards, low, high):
    level, own = 1.0, jax.random.fold_in(key, 6)
    for dim, shards_of in shards:
        steps = jnp.exp(jax.random.uniform(jax.random.fold_in(own, dim), (shards_of,), jnp.float32, low / len(shards), high / len(shards)))
        level = level * jnp.repeat(steps, extent[dim] // shards_of).reshape([-1 if axis == dim else 1 for axis in range(len(extent))])
    return level


def noise(key, dims, deviation, most, pieces=(), kind=jnp.bfloat16):
    result = jax.random.normal(key, dims, jnp.float32) * deviation
    if len(pieces) > 0:
        result = shard_levels(key, dims, pieces, -0.22, 0.18) * result
    return jnp.clip(result, min=-most, max=most).astype(kind)


def heavy_noise(rng, extent, width, most, cuts, heavy, kind=jnp.bfloat16):
    values = width * jax.random.normal(rng, extent, jnp.float32)
    if cuts:
        values = values * shard_levels(rng, extent, cuts, -0.22, 0.18)
    return jnp.clip(raised(values, jax.random.fold_in(rng, 3), *heavy), -most, most).astype(kind)


def setup_inputs(seed: int = 0) -> dict:
    seeds = jax.random.split(jax.random.key(seed), 7)
    return {
        "student_input": heavy_noise(seeds[0], (TOKENS, D), 1.0, 6.0, ((0, 16), (1, 16)), (0, 1, 16, 2.0)),
        "teacher_hidden": draw_teacher_hidden(jax.random.fold_in(seeds[6], 71), 0),
        "projector": heavy_noise(seeds[2], (TW, D), TW ** -0.5, 0.0625, ((0, 16), (1, 16)), (0, 1, 16, 2.0)),
        "gate_weight": noise(seeds[3], (FW, D), D ** -0.5, 0.09375, ((0, 16),)),
        "up_weight": noise(seeds[4], (FW, D), D ** -0.5, 0.09375, ((0, 16),)),
        "down_weight": noise(seeds[5], (FW, D), FW ** -0.5, 0.0625, ((0, 16),)),
    }


epsilon = 1e-05

def silu_parts(gate_val):
    sigma = jax.nn.sigmoid(gate_val)
    return (gate_val * sigma, sigma * (1.0 + gate_val * (1.0 - sigma)))

def contract_rows(left, right):
    return lax.dot_general(left, right, (((0,), (0,)), ((), ())), preferred_element_type=jnp.float32)

def contract_cols(left, right):
    return lax.dot_general(left, right, (((1,), (1,)), ((), ())), preferred_element_type=jnp.float32)

def reference(student_input, teacher_hidden, projector, gate_weight, up_weight, down_weight):
    stream = student_input.astype(jnp.float32)
    gate_val = contract_cols(student_input, gate_weight)
    up_val = contract_cols(student_input, up_weight)
    activated, slope_val = silu_parts(gate_val)
    hidden = (activated * up_val).astype(jnp.bfloat16)
    stream = stream + jnp.dot(hidden, down_weight, preferred_element_type=jnp.float32)
    projected = jnp.dot(teacher_hidden, projector, preferred_element_type=jnp.float32)
    teacher_float = teacher_hidden.astype(jnp.float32)
    mean_square = lax.optimization_barrier(jnp.sum(teacher_float * teacher_float, axis=1)) / TW
    target = projected / jnp.sqrt(mean_square + epsilon)[:, None]
    mismatch = stream - target
    loss_value = 0.5 * jnp.sum(mismatch * mismatch) / TOKENS
    grad_out = (mismatch / TOKENS).astype(jnp.bfloat16)
    grad_down = contract_rows(hidden, grad_out)
    grad_hidden = contract_cols(grad_out, down_weight)
    grad_gate_in = (grad_hidden * up_val * slope_val).astype(jnp.bfloat16)
    grad_up_in = (grad_hidden * activated).astype(jnp.bfloat16)
    grad_gate = contract_rows(grad_gate_in, student_input)
    grad_up = contract_rows(grad_up_in, student_input)
    return (loss_value, grad_gate, grad_up, grad_down)
```

```python
import jax
import jax.numpy as jnp
from jax import lax
from jax.sharding import PartitionSpec as P

epsilon = 1e-05

GROUP = ("sec", "tp")
EVERY = ("sec", "tp", "dp")
LINES = [[2 * z + c for z in range(8)] for c in range(2)]
SIBLING = [(d, d ^ 1) for d in range(16)]
SWAP = [
    (s * 16 + d, ((d & 14) | (s & 1)) * 16 + ((s & 14) | (d & 1)))
    for s in range(16)
    for d in range(16)
]


def silu_parts(gate_val):
    sigma = jax.nn.sigmoid(gate_val)
    return (gate_val * sigma, sigma * (1.0 + gate_val * (1.0 - sigma)))


def contract_rows(left, right):
    return lax.dot_general(
        left, right, (((0,), (0,)), ((), ())), preferred_element_type=jnp.float32
    )


def contract_cols(left, right):
    return lax.dot_general(
        left, right, (((1,), (1,)), ((), ())), preferred_element_type=jnp.float32
    )


def gather_group(block):
    copies = jnp.broadcast_to(block[None], (16,) + block.shape)
    return lax.all_to_all(copies, GROUP, 0, 0, tiled=True)


def gather_line(block):
    copies = jnp.broadcast_to(block[None], (8,) + block.shape)
    return lax.all_to_all(copies, "dp", 0, 0, axis_index_groups=LINES, tiled=True)


def scatter_sum(parts):
    return jnp.sum(
        lax.all_to_all(parts, GROUP, 0, 0, tiled=True).astype(jnp.float32), axis=0
    )


def split3(value):
    high = lax.reduce_precision(value, 8, 7)
    mid = lax.reduce_precision(value - high, 8, 7)
    low = value - high - mid
    return jnp.stack([high, mid, low]).astype(jnp.bfloat16)


def with_rows(block, extra):
    columns = block.shape[1]
    rows = jnp.pad(split3(extra), ((0, 13), (0, columns - extra.shape[0])))
    return jnp.concatenate([block, rows], axis=0)


def rows_of(blocks, tokens, count):
    rows = blocks[:, tokens : tokens + 3, :count].astype(jnp.float32)
    return jnp.sum(jnp.sum(rows, axis=1), axis=0)


def shards(student_input, teacher_hidden, projector, gate_weight, up_weight, down_weight):
    tokens, width = student_input.shape
    units = gate_weight.shape[0]
    tokens_all = tokens * 16
    teacher_units = teacher_hidden.shape[1] * 16
    core = lax.rem(lax.axis_index("dp"), 2)

    teacher_lines = lax.all_gather(
        teacher_hidden, "dp", axis=0, axis_index_groups=LINES, tiled=True
    )
    projector_other = lax.ppermute(projector, "dp", SIBLING)
    teacher_float = teacher_hidden.astype(jnp.float32)
    squares = jnp.sum(teacher_float * teacher_float, axis=1)

    gathered = gather_group(with_rows(student_input, squares))
    row_total = rows_of(gathered, tokens, tokens)
    inputs_full = gathered[:, :tokens].transpose(1, 0, 2).reshape(tokens, 16 * width)
    inputs_swapped = gather_group(lax.ppermute(student_input, EVERY, SWAP))

    gate_val = contract_cols(inputs_full, gate_weight)
    up_val = contract_cols(inputs_full, up_weight)
    activated, slope_val = silu_parts(gate_val)
    hidden = (activated * up_val).astype(jnp.bfloat16)
    gates = jnp.concatenate(
        [hidden, (up_val * slope_val).astype(jnp.bfloat16), activated.astype(jnp.bfloat16)],
        axis=1,
    )
    gates_lines = lax.all_gather(gates, "dp", axis=0, axis_index_groups=LINES, tiled=True)

    down_part = lax.dot_general(
        hidden,
        down_weight,
        (((1,), (0,)), ((), ())),
        preferred_element_type=jnp.float32,
    )
    down_part = down_part.reshape(tokens, 16, width).transpose(1, 0, 2).astype(jnp.bfloat16)
    stream = student_input.astype(jnp.float32) + scatter_sum(down_part)

    pair = jnp.where(
        core == 0,
        jnp.concatenate([projector, projector_other], axis=1),
        jnp.concatenate([projector_other, projector], axis=1),
    )
    projected = jnp.dot(teacher_lines, pair, preferred_element_type=jnp.float32)
    projected = projected.reshape(8, tokens, 2, width).transpose(0, 2, 1, 3)
    projected = projected.reshape(16, tokens, width).astype(jnp.bfloat16)
    target_part = lax.ppermute(scatter_sum(projected), EVERY, SWAP)
    target = target_part / jnp.sqrt(row_total / teacher_units + epsilon)[:, None]

    mismatch = stream - target
    summed_loss = jnp.sum(mismatch * mismatch)
    outgrad_part = (mismatch / tokens_all).astype(jnp.bfloat16)
    outgrad_gathered = gather_group(with_rows(outgrad_part, summed_loss[None]))
    group_loss = rows_of(outgrad_gathered, tokens, 1)
    outgrad_full = outgrad_gathered[:, :tokens].transpose(1, 0, 2).reshape(tokens, 16 * width)
    outgrad_swapped = gather_group(lax.ppermute(outgrad_part, EVERY, SWAP))

    grad_hidden = contract_cols(outgrad_full, down_weight).astype(jnp.bfloat16)
    hidden_gathered = gather_line(with_rows(grad_hidden, group_loss))
    line_loss = rows_of(hidden_gathered, tokens, 1)
    grad_hidden_lines = hidden_gathered[:, :tokens].reshape(8 * tokens, units).astype(jnp.float32)

    hidden_lines = gates_lines[:, :units]
    gate_lines = (grad_hidden_lines * gates_lines[:, units : 2 * units].astype(jnp.float32)).astype(
        jnp.bfloat16
    )
    up_lines = (grad_hidden_lines * gates_lines[:, 2 * units :].astype(jnp.float32)).astype(
        jnp.bfloat16
    )

    def columns_of(swapped):
        swapped = swapped.reshape(8, 2, tokens, width).transpose(0, 2, 1, 3)
        return swapped.reshape(8 * tokens, 2 * width)

    def finish(left, right):
        both = contract_rows(left, right)
        low, high = both[:, :width], both[:, width:]
        mine, theirs = jnp.where(core == 0, low, high), jnp.where(core == 0, high, low)
        return mine + lax.ppermute(theirs, "dp", SIBLING)

    grad_down = finish(hidden_lines, columns_of(outgrad_swapped))
    grad_gate = finish(gate_lines, columns_of(inputs_swapped))
    grad_up = finish(up_lines, columns_of(inputs_swapped))
    all_loss = line_loss + lax.ppermute(line_loss, "dp", SIBLING)
    loss_value = 0.5 * all_loss[0] / tokens_all
    return (loss_value, grad_gate, grad_up, grad_down)


def solution(mesh):
    in_specs = (
        P("dp", ("sec", "tp")),
        P("dp", ("sec", "tp")),
        P(("sec", "tp"), "dp"),
        P(("sec", "tp"), None),
        P(("sec", "tp"), None),
        P(("sec", "tp"), None),
    )
    out_specs = (P(), P(("sec", "tp"), "dp"), P(("sec", "tp"), "dp"), P(("sec", "tp"), "dp"))
    return jax.shard_map(shards, mesh=mesh, in_specs=in_specs, out_specs=out_specs, check_vma=False)
```

```python
import functools

import jax
import jax.numpy as jnp
from jax import lax
from jax.experimental import pallas as pl
from jax.experimental.pallas import tpu as pltpu
from jax.sharding import PartitionSpec as P

epsilon = 1e-05

GROUP = ("sec", "tp")
EVERY = ("sec", "tp", "dp")
LINES = [[2 * z + c for z in range(8)] for c in range(2)]
SIBLING = [(d, d ^ 1) for d in range(16)]
SWAP = [
    (s * 16 + d, ((d & 14) | (s & 1)) * 16 + ((s & 14) | (d & 1)))
    for s in range(16)
    for d in range(16)
]


def silu_parts(gate_val):
    sigma = jax.nn.sigmoid(gate_val)
    return (gate_val * sigma, sigma * (1.0 + gate_val * (1.0 - sigma)))


def contract_cols(left, right):
    return lax.dot_general(
        left, right, (((1,), (1,)), ((), ())), preferred_element_type=jnp.float32
    )


def gather_group(block):
    copies = jnp.broadcast_to(block[None], (16,) + block.shape)
    return lax.all_to_all(copies, GROUP, 0, 0, tiled=True)


RIGHT = [(d, (d + 2) % 16) for d in range(16)]
LEFT = [(d, (d - 2) % 16) for d in range(16)]


def ring(block, chains=1, hold=None):
    rows = block.shape[0] // chains
    half = rows // 2
    found = [[] for _ in range(8)]
    heads = []
    for chain in range(chains):
        up = down = block[chain * rows : (chain + 1) * rows]
        found[0].append((chain * rows, up))
        heads.append((up, down))
    for step in range(1, 5):
        if step == 4 and hold is not None:
            heads, _ = lax.optimization_barrier((heads, hold))
        if step == 4:
            heads = [(up[:half], down[half:]) for up, down in heads]
        heads = [(lax.ppermute(up, "dp", RIGHT), lax.ppermute(down, "dp", LEFT)) for up, down in heads]
        for chain, (up, down) in enumerate(heads):
            if step == 4:
                found[4] += [(chain * rows, up), (chain * rows + half, down)]
            else:
                found[-step].append((chain * rows, up))
                found[step].append((chain * rows, down))
    return found


def fetch(pairs, sems):
    copies = [pltpu.make_async_copy(src, dst, sems.at[i]) for i, (src, dst) in enumerate(pairs)]
    for copy in copies:
        copy.start()
    return copies


def down_kernel(place_ref, hidden_ref, down_ref, out_ref):
    width = out_ref.shape[2]
    for i in range(8):
        columns = pl.ds(pl.multiple_of((2 * i + place_ref[1]) * width, width), width)
        out_ref[i] = lax.dot_general(
            hidden_ref[...],
            down_ref[:, columns],
            (((0,), (0,)), ((), ())),
            preferred_element_type=jnp.float32,
        )


def parts_kernel(tokens, teacher_ref, scale_ref, down_ref, line_hbm, *refs):
    mine_ref, other_ref, line_ref, sems = refs
    copies = fetch([(line_hbm.at[i], line_ref.at[i]) for i in range(8)], sems)
    for i in range(8):
        copies[i].wait()
        projected = jnp.dot(teacher_ref[...], line_ref[i], preferred_element_type=jnp.float32)
        part = (down_ref[i] - scale_ref[...] * projected).astype(jnp.bfloat16)
        mine_ref[i] = part[:tokens]
        other_ref[i] = part[tokens:]


def grads_kernel(tokens, place_ref, gates_hbm, inputs_hbm, outgrads_hbm, *refs):
    blocks, mine_refs, theirs_ref = refs[:8], refs[8:11], refs[11]
    gates_ref, inputs_ref, outgrads_ref, block_ref, lefts_ref, sems = refs[12:]
    start, core = place_ref[0], place_ref[1]
    units = lefts_ref.shape[1]
    pairs = [(blocks[i].at[pl.ds(0, units)], block_ref.at[i]) for i in range(8)]
    pairs += [(inputs_hbm, inputs_ref), (outgrads_hbm, outgrads_ref)]
    copies = fetch([(gates_hbm, gates_ref)] + pairs, sems)
    copies[0].wait()
    for i in range(8):
        spot = lax.rem(start + i, 8)
        columns = pl.ds(i * tokens, tokens)
        gate, up = gates_ref[spot, :units], gates_ref[spot, units:]
        copies[1 + i].wait()
        grad_hidden = block_ref[i].astype(jnp.float32)
        activated, slope = silu_parts(gate)
        lefts_ref[0, :, columns] = (grad_hidden * up * slope).astype(jnp.bfloat16)
        lefts_ref[1, :, columns] = (grad_hidden * activated).astype(jnp.bfloat16)
        lefts_ref[2, :, columns] = (activated * up).astype(jnp.bfloat16)
    copies[9].wait()
    copies[10].wait()

    def rows(ref, half):
        return jnp.concatenate(
            [ref[2 * lax.rem(start + i, 8) + half] for i in range(8)], axis=0
        )

    for mine, half in ((False, 1 - core), (True, core)):
        inputs, outgrads = rows(inputs_ref, half), rows(outgrads_ref, half)
        for part, right in enumerate((inputs, inputs, outgrads)):
            found = jnp.dot(lefts_ref[part], right, preferred_element_type=jnp.float32)
            if mine:
                mine_refs[part][...] = found
            else:
                theirs_ref[part] = found


def scatter_sum(parts):
    return jnp.sum(
        lax.all_to_all(parts, GROUP, 0, 0, tiled=True).astype(jnp.float32), axis=0
    )


def split3(value):
    high = lax.reduce_precision(value, 8, 7)
    mid = lax.reduce_precision(value - high, 8, 7)
    low = value - high - mid
    return jnp.stack([high, mid, low]).astype(jnp.bfloat16)


def with_rows(block, extra):
    columns = block.shape[1]
    rows = jnp.pad(split3(extra), ((0, 13), (0, columns - extra.shape[0])))
    return jnp.concatenate([block, rows], axis=0)


def rows_of(blocks, tokens, count):
    rows = blocks[:, tokens : tokens + 3, :count].astype(jnp.float32)
    return jnp.sum(jnp.sum(rows, axis=1), axis=0)


def shards(student_input, teacher_hidden, projector, gate_weight, up_weight, down_weight):
    tokens, width = student_input.shape
    units = gate_weight.shape[0]
    tokens_all = tokens * 16
    teacher_units = teacher_hidden.shape[1] * 16
    place = lax.axis_index("dp")
    core = lax.rem(place, 2)
    start = lax.div(place, 2)
    where = jnp.stack([start, core])
    vmem, anywhere = pl.BlockSpec(memory_space=pltpu.VMEM), pl.BlockSpec(memory_space=pl.ANY)
    smem = pl.BlockSpec(memory_space=pltpu.SMEM)

    projector_line = lax.all_gather(projector, "dp", axis=0, axis_index_groups=LINES)
    inputs_moved = lax.ppermute(student_input, EVERY, SWAP)
    teacher_pair = jnp.concatenate(
        [teacher_hidden, lax.ppermute(teacher_hidden, "dp", SIBLING)], axis=0
    )
    teacher_float = teacher_hidden.astype(jnp.float32)
    squares = jnp.sum(teacher_float * teacher_float, axis=1)

    gathered = gather_group(with_rows(student_input, squares))
    inputs_moved, _ = lax.optimization_barrier((inputs_moved, gathered))
    inputs_swapped = gather_group(inputs_moved)
    row_total = rows_of(gathered, tokens, tokens)
    row_scale = 1.0 / jnp.sqrt(row_total / teacher_units + epsilon)
    scale_pair = jnp.concatenate([row_scale, lax.ppermute(row_scale, "dp", SIBLING)])[:, None]
    inputs_full = gathered[:, :tokens].transpose(1, 0, 2).reshape(tokens, 16 * width)

    gate_val = contract_cols(gate_weight, inputs_full)
    up_val = contract_cols(up_weight, inputs_full)
    hidden = (silu_parts(gate_val)[0] * up_val).astype(jnp.bfloat16)
    hidden_pair = jnp.concatenate([hidden, lax.ppermute(hidden, "dp", SIBLING)], axis=1)

    down_part = pl.pallas_call(
        down_kernel,
        out_shape=jax.ShapeDtypeStruct((8, 2 * tokens, width), jnp.float32),
        in_specs=[smem, vmem, vmem],
        out_specs=vmem,
        compiler_params=pltpu.CompilerParams(vmem_limit_bytes=16 * 2**20),
        cost_estimate=pl.CostEstimate(
            flops=2 * 256 * 448 * 2048, bytes_accessed=6 * 2**20, transcendentals=0
        ),
    )(where, hidden_pair, down_weight)
    part = jax.ShapeDtypeStruct((8, tokens, width), jnp.bfloat16)
    mine, other = pl.pallas_call(
        functools.partial(parts_kernel, tokens),
        out_shape=(part, part),
        in_specs=[vmem, vmem, vmem, anywhere],
        out_specs=(vmem, vmem),
        scratch_shapes=[
            pltpu.VMEM(projector_line.shape, jnp.bfloat16),
            pltpu.SemaphoreType.DMA((8,)),
        ],
        compiler_params=pltpu.CompilerParams(vmem_limit_bytes=56 * 2**20),
        cost_estimate=pl.CostEstimate(
            flops=2 * 256 * 2048 * 1024, bytes_accessed=6 * 2**20, transcendentals=0
        ),
    )(teacher_pair, scale_pair, down_part, projector_line)
    other = lax.ppermute(other, "dp", SIBLING)
    parts = jnp.stack(
        [jnp.where(core == 0, mine, other), jnp.where(core == 0, other, mine)], axis=1
    ).reshape(16, tokens, width)
    gates = jnp.concatenate([gate_val, up_val], axis=0)
    gates, parts, inputs_swapped = lax.optimization_barrier((gates, parts, inputs_swapped))
    gates_line = lax.all_gather(gates, "dp", axis=0, axis_index_groups=LINES)
    mismatch = student_input.astype(jnp.float32) + scatter_sum(parts)

    row_loss = jnp.sum(mismatch * mismatch, axis=1)
    outgrad_part = (mismatch / tokens_all).astype(jnp.bfloat16)
    outgrad_gathered = gather_group(with_rows(outgrad_part, row_loss))
    group_loss = rows_of(outgrad_gathered, tokens, tokens)
    outgrad_full = outgrad_gathered[:, :tokens].transpose(1, 0, 2).reshape(tokens, 16 * width)
    outgrad_moved = lax.ppermute(outgrad_part, EVERY, SWAP)

    grad_hidden = contract_cols(down_weight, outgrad_full).astype(jnp.bfloat16)
    outgrad_moved, _ = lax.optimization_barrier((outgrad_moved, grad_hidden))
    outgrad_swapped = gather_group(outgrad_moved)
    line = ring(jnp.pad(with_rows(grad_hidden, group_loss), ((0, 16), (0, 0))))
    line = [jnp.concatenate([piece for _, piece in found], axis=0) for found in line]
    line_loss = rows_of(jnp.stack([found[units : units + 16] for found in line]), 0, tokens)

    grad = jax.ShapeDtypeStruct((units, width), jnp.float32)
    *mine, theirs = pl.pallas_call(
        functools.partial(grads_kernel, tokens),
        out_shape=(grad, grad, grad, jax.ShapeDtypeStruct((3, units, width), jnp.float32)),
        in_specs=[smem] + [anywhere] * 11,
        out_specs=(vmem,) * 4,
        scratch_shapes=[
            pltpu.VMEM(gates_line.shape, jnp.float32),
            pltpu.VMEM(inputs_swapped.shape, jnp.bfloat16),
            pltpu.VMEM(outgrad_swapped.shape, jnp.bfloat16),
            pltpu.VMEM((8, units, tokens), jnp.bfloat16),
            pltpu.VMEM((3, units, 8 * tokens), jnp.bfloat16),
            pltpu.SemaphoreType.DMA((11,)),
        ],
        compiler_params=pltpu.CompilerParams(vmem_limit_bytes=60 * 2**20),
        cost_estimate=pl.CostEstimate(
            flops=2 * 3 * 1024 * 448 * 512, bytes_accessed=10 * 2**20, transcendentals=2**19
        ),
    )(where, gates_line, inputs_swapped, outgrad_swapped, *line)
    theirs = lax.ppermute(theirs, "dp", SIBLING)
    grad_gate, grad_up, grad_down = [mine[part] + theirs[part] for part in range(3)]
    all_loss = line_loss + lax.ppermute(line_loss, "dp", SIBLING)
    loss_value = 0.5 * jnp.sum(all_loss) / tokens_all
    return (loss_value, grad_gate, grad_up, grad_down)


def solution(mesh):
    in_specs = (
        P("dp", ("sec", "tp")),
        P("dp", ("sec", "tp")),
        P(("sec", "tp"), "dp"),
        P(("sec", "tp"), None),
        P(("sec", "tp"), None),
        P(("sec", "tp"), None),
    )
    out_specs = (P(), P(("sec", "tp"), "dp"), P(("sec", "tp"), "dp"), P(("sec", "tp"), "dp"))
    return jax.shard_map(shards, mesh=mesh, in_specs=in_specs, out_specs=out_specs, check_vma=False)
```

```python
import functools

import jax
import jax.numpy as jnp
from jax import lax
from jax.experimental import pallas as pl
from jax.experimental.pallas import tpu as pltpu
from jax.sharding import PartitionSpec as P

epsilon = 1e-05

GROUP = ("sec", "tp")
EVERY = ("sec", "tp", "dp")
LINES = [[2 * z + c for z in range(8)] for c in range(2)]
SIBLING = [(d, d ^ 1) for d in range(16)]
SWAP = [
    (s * 16 + d, ((d & 14) | (s & 1)) * 16 + ((s & 14) | (d & 1)))
    for s in range(16)
    for d in range(16)
]


def silu_parts(gate_val):
    sigma = jax.nn.sigmoid(gate_val)
    return (gate_val * sigma, sigma * (1.0 + gate_val * (1.0 - sigma)))


def contract_cols(left, right):
    return lax.dot_general(
        left, right, (((1,), (1,)), ((), ())), preferred_element_type=jnp.float32
    )


def gather_group(block):
    copies = jnp.broadcast_to(block[None], (16,) + block.shape)
    return lax.all_to_all(copies, GROUP, 0, 0, tiled=True)


RIGHT = [(d, (d + 2) % 16) for d in range(16)]
LEFT = [(d, (d - 2) % 16) for d in range(16)]


def ring(block):
    half = block.shape[0] // 2
    up = down = block
    found = [[(0, block)]] + [[] for _ in range(7)]
    for step in range(1, 4):
        up, down = lax.ppermute(up, "dp", RIGHT), lax.ppermute(down, "dp", LEFT)
        found[-step], found[step] = [(0, up)], [(0, down)]
    up, down = lax.ppermute(up[:half], "dp", RIGHT), lax.ppermute(down[half:], "dp", LEFT)
    found[4] = [(0, up), (half, down)]
    return found


def fetch(pairs, sems):
    copies = [pltpu.make_async_copy(src, dst, sems.at[i]) for i, (src, dst) in enumerate(pairs)]
    for copy in copies:
        copy.start()
    return copies


def down_kernel(place_ref, hidden_ref, down_ref, out_ref):
    width = out_ref.shape[2]
    for i in range(8):
        columns = pl.ds(pl.multiple_of((2 * i + place_ref[1]) * width, width), width)
        out_ref[i] = lax.dot_general(
            hidden_ref[...],
            down_ref[:, columns],
            (((0,), (0,)), ((), ())),
            preferred_element_type=jnp.float32,
        )


def hidden_kernel(tokens, blocks_ref, down_ref, out_ref):
    width = blocks_ref.shape[2]
    total = None
    for i in range(16):
        found = contract_cols(down_ref[:, i * width : (i + 1) * width], blocks_ref[i, :tokens])
        total = found if total is None else total + found
    out_ref[...] = total.astype(out_ref.dtype)


def columns_of(ref, half, start):
    return jnp.concatenate(
        [ref[2 * lax.rem(start + i, 8) + half] for i in range(8)], axis=0
    )


def grads_kernel(tokens, spans, place_ref, gates_hbm, inputs_hbm, outgrads_hbm, *refs):
    count = sum(len(span) for span in spans)
    blocks, mine_refs, theirs_ref = refs[:count], refs[count : count + 3], refs[count + 3]
    gates_ref, inputs_ref, outgrads_ref, block_ref, lefts_ref, sems = refs[count + 4 :]
    start, core = place_ref[0], place_ref[1]
    units = lefts_ref.shape[1]
    spots = [lax.rem(start + i, 8) for i in range(8)]
    pieces = iter(blocks)
    pairs = []
    for i, span in enumerate(spans):
        pairs.append((gates_hbm.at[spots[i]], gates_ref.at[i]))
        for first, rows in span:
            source = next(pieces).at[pl.ds(0, rows)]
            pairs.append((source, block_ref.at[i, pl.ds(first, rows)]))
    pairs += [(inputs_hbm, inputs_ref), (outgrads_hbm, outgrads_ref)]
    waiting = iter(fetch(pairs, sems))
    for i in range(8):
        for _ in range(1 + len(spans[i])):
            next(waiting).wait()
        columns = pl.ds(i * tokens, tokens)
        gate, up = gates_ref[i, :units], gates_ref[i, units:]
        grad_hidden = block_ref[i].astype(jnp.float32)
        activated, slope = silu_parts(gate)
        lefts_ref[0, :, columns] = (grad_hidden * up * slope).astype(jnp.bfloat16)
        lefts_ref[1, :, columns] = (grad_hidden * activated).astype(jnp.bfloat16)
        lefts_ref[2, :, columns] = (activated * up).astype(jnp.bfloat16)
    for copy in waiting:
        copy.wait()
    for mine, half in ((False, 1 - core), (True, core)):
        inputs = columns_of(inputs_ref, half, start)
        outgrads = columns_of(outgrads_ref, half, start)
        for part, right in enumerate((inputs, inputs, outgrads)):
            found = jnp.dot(lefts_ref[part], right, preferred_element_type=jnp.float32)
            if mine:
                mine_refs[part][...] = found
            else:
                theirs_ref[part] = found


def scatter_sum(parts):
    return jnp.sum(
        lax.all_to_all(parts, GROUP, 0, 0, tiled=True).astype(jnp.float32), axis=0
    )


def split3(value):
    high = lax.reduce_precision(value, 8, 7)
    mid = lax.reduce_precision(value - high, 8, 7)
    low = value - high - mid
    return jnp.stack([high, mid, low]).astype(jnp.bfloat16)


def with_rows(block, extra):
    columns = block.shape[1]
    rows = jnp.pad(split3(extra), ((0, 5), (0, columns - extra.shape[0])))
    return jnp.concatenate([block, rows], axis=0)


def rows_of(blocks, tokens, count):
    rows = blocks[:, tokens : tokens + 3, :count].astype(jnp.float32)
    return jnp.sum(jnp.sum(rows, axis=1), axis=0)


def shards(student_input, teacher_hidden, projector, gate_weight, up_weight, down_weight):
    tokens, width = student_input.shape
    units = gate_weight.shape[0]
    tokens_all = tokens * 16
    teacher_units = teacher_hidden.shape[1] * 16
    place = lax.axis_index("dp")
    core = lax.rem(place, 2)
    start = lax.div(place, 2)
    where = jnp.stack([start, core])
    vmem, anywhere = pl.BlockSpec(memory_space=pltpu.VMEM), pl.BlockSpec(memory_space=pl.ANY)
    smem = pl.BlockSpec(memory_space=pltpu.SMEM)

    projector_line = lax.all_gather(projector, "dp", axis=0, axis_index_groups=LINES)
    inputs_moved = lax.ppermute(student_input, EVERY, SWAP)
    teacher_pair = jnp.concatenate(
        [teacher_hidden, lax.ppermute(teacher_hidden, "dp", SIBLING)], axis=0
    )
    teacher_float = teacher_hidden.astype(jnp.float32)
    squares = jnp.sum(teacher_float * teacher_float, axis=1)

    gathered = gather_group(with_rows(student_input, squares))
    inputs_moved, _ = lax.optimization_barrier((inputs_moved, gathered))
    inputs_swapped = gather_group(inputs_moved)
    row_total = rows_of(gathered, tokens, tokens)
    row_scale = 1.0 / jnp.sqrt(row_total / teacher_units + epsilon)
    scale_pair = jnp.concatenate([row_scale, lax.ppermute(row_scale, "dp", SIBLING)])[:, None]
    inputs_full = gathered[:, :tokens].transpose(1, 0, 2).reshape(tokens, 16 * width)

    gate_val = contract_cols(gate_weight, inputs_full)
    up_val = contract_cols(up_weight, inputs_full)
    hidden = (silu_parts(gate_val)[0] * up_val).astype(jnp.bfloat16)
    hidden_pair = jnp.concatenate([hidden, lax.ppermute(hidden, "dp", SIBLING)], axis=1)

    down_part = pl.pallas_call(
        down_kernel,
        out_shape=jax.ShapeDtypeStruct((8, 2 * tokens, width), jnp.float32),
        in_specs=[smem, vmem, vmem],
        out_specs=vmem,
        compiler_params=pltpu.CompilerParams(vmem_limit_bytes=16 * 2**20),
        cost_estimate=pl.CostEstimate(
            flops=2 * 256 * 448 * 2048, bytes_accessed=6 * 2**20, transcendentals=0
        ),
    )(where, hidden_pair, down_weight)
    projected = jnp.einsum(
        "tk,zkn->ztn",
        teacher_pair,
        projector_line,
        preferred_element_type=jnp.float32,
    )
    part = (down_part - projected * scale_pair).astype(jnp.bfloat16)
    mine, other = part[:, :tokens], part[:, tokens:]
    other = lax.ppermute(other, "dp", SIBLING)
    parts = jnp.stack(
        [jnp.where(core == 0, mine, other), jnp.where(core == 0, other, mine)], axis=1
    ).reshape(16, tokens, width)
    gates = jnp.concatenate([gate_val, up_val], axis=0)
    gates, parts, inputs_swapped = lax.optimization_barrier((gates, parts, inputs_swapped))
    gates_line = lax.all_gather(gates, "dp", axis=0, axis_index_groups=LINES)
    mismatch = student_input.astype(jnp.float32) + scatter_sum(parts)

    row_loss = jnp.sum(mismatch * mismatch, axis=1)
    outgrad_part = (mismatch / tokens_all).astype(jnp.bfloat16)
    outgrad_gathered = gather_group(with_rows(outgrad_part, row_loss))
    group_loss = rows_of(outgrad_gathered, tokens, tokens)
    outgrad_moved = lax.ppermute(outgrad_part, EVERY, SWAP)

    grad_hidden = pl.pallas_call(
        functools.partial(hidden_kernel, tokens),
        out_shape=jax.ShapeDtypeStruct((units, tokens), jnp.bfloat16),
        in_specs=[vmem, vmem],
        out_specs=vmem,
        compiler_params=pltpu.CompilerParams(vmem_limit_bytes=16 * 2**20),
        cost_estimate=pl.CostEstimate(
            flops=2 * 128 * 448 * 4096, bytes_accessed=5 * 2**20, transcendentals=0
        ),
    )(outgrad_gathered, down_weight)
    outgrad_moved, _ = lax.optimization_barrier((outgrad_moved, grad_hidden))
    outgrad_swapped = gather_group(outgrad_moved)
    line = ring(jnp.pad(with_rows(grad_hidden, group_loss), ((0, 24), (0, 0))))
    line_loss = jnp.stack([found[-1][1][units - found[-1][0] :] for found in line])
    line_loss = rows_of(line_loss, 0, tokens)
    spans = [[(first, min(piece.shape[0], units - first)) for first, piece in found] for found in line]
    pieces = [piece for found in line for _, piece in found]

    grad = jax.ShapeDtypeStruct((units, width), jnp.float32)
    *mine, theirs = pl.pallas_call(
        functools.partial(grads_kernel, tokens, spans),
        out_shape=(grad, grad, grad, jax.ShapeDtypeStruct((3, units, width), jnp.float32)),
        in_specs=[smem] + [anywhere] * (3 + len(pieces)),
        out_specs=(vmem,) * 4,
        scratch_shapes=[
            pltpu.VMEM(gates_line.shape, jnp.float32),
            pltpu.VMEM(inputs_swapped.shape, jnp.bfloat16),
            pltpu.VMEM(outgrad_swapped.shape, jnp.bfloat16),
            pltpu.VMEM((8, units, tokens), jnp.bfloat16),
            pltpu.VMEM((3, units, 8 * tokens), jnp.bfloat16),
            pltpu.SemaphoreType.DMA((10 + len(pieces),)),
        ],
        compiler_params=pltpu.CompilerParams(vmem_limit_bytes=60 * 2**20),
        cost_estimate=pl.CostEstimate(
            flops=2 * 3 * 1024 * 448 * 512, bytes_accessed=10 * 2**20, transcendentals=2**19
        ),
    )(where, gates_line, inputs_swapped, outgrad_swapped, *pieces)
    theirs = lax.ppermute(theirs, "dp", SIBLING)
    grad_gate, grad_up, grad_down = [mine[part] + theirs[part] for part in range(3)]
    all_loss = line_loss + lax.ppermute(line_loss, "dp", SIBLING)
    loss_value = 0.5 * jnp.sum(all_loss) / tokens_all
    return (loss_value, grad_gate, grad_up, grad_down)


def solution(mesh):
    in_specs = (
        P("dp", ("sec", "tp")),
        P("dp", ("sec", "tp")),
        P(("sec", "tp"), "dp"),
        P(("sec", "tp"), None),
        P(("sec", "tp"), None),
        P(("sec", "tp"), None),
    )
    out_specs = (P(), P(("sec", "tp"), "dp"), P(("sec", "tp"), "dp"), P(("sec", "tp"), "dp"))
    return jax.shard_map(shards, mesh=mesh, in_specs=in_specs, out_specs=out_specs, check_vma=False)
```

```python
import functools

import jax
import jax.numpy as jnp
from jax import lax
from jax.experimental import pallas as pl
from jax.experimental.pallas import tpu as pltpu
from jax.sharding import PartitionSpec as P

epsilon = 1e-05

GROUP = ("sec", "tp")
EVERY = ("sec", "tp", "dp")
LINES = [[2 * z + c for z in range(8)] for c in range(2)]
SIBLING = [(d, d ^ 1) for d in range(16)]
SWAP = [
    (s * 16 + d, ((d & 14) | (s & 1)) * 16 + ((s & 14) | (d & 1)))
    for s in range(16)
    for d in range(16)
]


def silu_parts(gate_val):
    sigma = jax.nn.sigmoid(gate_val)
    return (gate_val * sigma, sigma * (1.0 + gate_val * (1.0 - sigma)))


def contract_cols(left, right):
    return lax.dot_general(
        left, right, (((1,), (1,)), ((), ())), preferred_element_type=jnp.float32
    )


def gather_group(block):
    copies = jnp.broadcast_to(block[None], (16,) + block.shape)
    return lax.all_to_all(copies, GROUP, 0, 0, tiled=True)


RIGHT = [(d, (d + 2) % 16) for d in range(16)]
LEFT = [(d, (d - 2) % 16) for d in range(16)]


def ring(block):
    half = block.shape[0] // 2
    up = down = block
    found = [[(0, block)]] + [[] for _ in range(7)]
    for step in range(1, 4):
        up, down = lax.ppermute(up, "dp", RIGHT), lax.ppermute(down, "dp", LEFT)
        found[-step], found[step] = [(0, up)], [(0, down)]
    up, down = lax.ppermute(up[:half], "dp", RIGHT), lax.ppermute(down[half:], "dp", LEFT)
    found[4] = [(0, up), (half, down)]
    return found


def fetch(pairs, sems):
    copies = [pltpu.make_async_copy(src, dst, sems.at[i]) for i, (src, dst) in enumerate(pairs)]
    for copy in copies:
        copy.start()
    return copies


def down_kernel(place_ref, hidden_ref, down_ref, out_ref):
    width = out_ref.shape[2]
    for i in range(8):
        columns = pl.ds(pl.multiple_of((2 * i + place_ref[1]) * width, width), width)
        out_ref[i] = lax.dot_general(
            hidden_ref[...],
            down_ref[:, columns],
            (((0,), (0,)), ((), ())),
            preferred_element_type=jnp.float32,
        )


def hidden_kernel(tokens, blocks_ref, down_ref, out_ref):
    width = blocks_ref.shape[2]
    units = down_ref.shape[0]
    total = loss = None
    for i in range(16):
        found = contract_cols(down_ref[:, i * width : (i + 1) * width], blocks_ref[i, :tokens])
        total = found if total is None else total + found
        rows = blocks_ref[i, tokens : tokens + 16, :tokens].astype(jnp.float32)
        loss = rows if loss is None else loss + rows
    out_ref[:units] = total.astype(out_ref.dtype)
    loss = jnp.sum(loss, axis=0, keepdims=True)
    high = loss.astype(jnp.bfloat16).astype(jnp.float32)
    mid = (loss - high).astype(jnp.bfloat16).astype(jnp.float32)
    low = loss - high - mid
    extra = (out_ref.shape[0] - units, tokens)
    row = lax.broadcasted_iota(jnp.int32, extra, 0)
    split = jnp.zeros(extra, jnp.float32)
    for i, value in enumerate((high, mid, low)):
        split = jnp.where(row == i, jnp.broadcast_to(value, extra), split)
    out_ref[units:] = split.astype(out_ref.dtype)


def columns_of(ref, half, start):
    return jnp.concatenate(
        [ref[2 * lax.rem(start + i, 8) + half] for i in range(8)], axis=0
    )


def grads_kernel(tokens, spans, place_ref, gates_hbm, inputs_hbm, outgrads_hbm, *refs):
    count = sum(len(span) for span in spans)
    blocks, theirs_refs, mine_ref = refs[:count], refs[count : count + 3], refs[count + 3]
    gates_ref, inputs_ref, outgrads_ref, block_ref, lefts_ref, sems = refs[count + 4 :]
    start, core = place_ref[0], place_ref[1]
    units = lefts_ref.shape[1]
    spots = [lax.rem(start + i, 8) for i in range(8)]
    pieces = iter(blocks)
    pairs = []
    for i, span in enumerate(spans):
        pairs.append((gates_hbm.at[spots[i]], gates_ref.at[i]))
        for first, rows in span:
            source = next(pieces).at[pl.ds(0, rows)]
            pairs.append((source, block_ref.at[i, pl.ds(first, rows)]))
    pairs += [(inputs_hbm, inputs_ref), (outgrads_hbm, outgrads_ref)]
    waiting = iter(fetch(pairs, sems))
    for i in range(8):
        for _ in range(1 + len(spans[i])):
            next(waiting).wait()
        columns = pl.ds(i * tokens, tokens)
        gate, up = gates_ref[i, :units], gates_ref[i, units:]
        grad_hidden = block_ref[i].astype(jnp.float32)
        activated, slope = silu_parts(gate)
        lefts_ref[0, :, columns] = (grad_hidden * up * slope).astype(jnp.bfloat16)
        lefts_ref[1, :, columns] = (grad_hidden * activated).astype(jnp.bfloat16)
        lefts_ref[2, :, columns] = (activated * up).astype(jnp.bfloat16)
    for copy in waiting:
        copy.wait()
    for mine, half in ((False, 1 - core), (True, core)):
        inputs = columns_of(inputs_ref, half, start)
        outgrads = columns_of(outgrads_ref, half, start)
        for part, right in enumerate((inputs, inputs, outgrads)):
            found = jnp.dot(lefts_ref[part], right, preferred_element_type=jnp.float32)
            if mine:
                mine_ref[part] = found
            else:
                theirs_refs[part][...] = found


def scatter_sum(parts):
    return jnp.sum(
        lax.all_to_all(parts, GROUP, 0, 0, tiled=True).astype(jnp.float32), axis=0
    )


def split3(value):
    high = lax.reduce_precision(value, 8, 7)
    mid = lax.reduce_precision(value - high, 8, 7)
    low = value - high - mid
    return jnp.stack([high, mid, low]).astype(jnp.bfloat16)


def with_rows(block, extra):
    columns = block.shape[1]
    rows = jnp.pad(split3(extra), ((0, 13), (0, columns - extra.shape[0])))
    return jnp.concatenate([block, rows], axis=0)


def rows_of(blocks, tokens, count):
    rows = blocks[:, tokens : tokens + 3, :count].astype(jnp.float32)
    return jnp.sum(jnp.sum(rows, axis=1), axis=0)


def shards(student_input, teacher_hidden, projector, gate_weight, up_weight, down_weight):
    tokens, width = student_input.shape
    units = gate_weight.shape[0]
    tokens_all = tokens * 16
    teacher_units = teacher_hidden.shape[1] * 16
    place = lax.axis_index("dp")
    core = lax.rem(place, 2)
    start = lax.div(place, 2)
    where = jnp.stack([start, core])
    vmem, anywhere = pl.BlockSpec(memory_space=pltpu.VMEM), pl.BlockSpec(memory_space=pl.ANY)
    smem = pl.BlockSpec(memory_space=pltpu.SMEM)

    projector_line = lax.all_gather(projector, "dp", axis=0, axis_index_groups=LINES)
    inputs_moved = lax.ppermute(student_input, EVERY, SWAP)
    teacher_pair = jnp.concatenate(
        [teacher_hidden, lax.ppermute(teacher_hidden, "dp", SIBLING)], axis=0
    )
    teacher_float = teacher_hidden.astype(jnp.float32)
    squares = jnp.sum(teacher_float * teacher_float, axis=1)

    gathered = gather_group(with_rows(student_input, squares))
    inputs_moved, _ = lax.optimization_barrier((inputs_moved, gathered))
    inputs_swapped = gather_group(inputs_moved)
    row_total = rows_of(gathered, tokens, tokens)
    row_scale = 1.0 / jnp.sqrt(row_total / teacher_units + epsilon)
    scale_pair = jnp.concatenate([row_scale, lax.ppermute(row_scale, "dp", SIBLING)])[:, None]
    inputs_full = gathered[:, :tokens].transpose(1, 0, 2).reshape(tokens, 16 * width)

    gate_val = contract_cols(gate_weight, inputs_full)
    up_val = contract_cols(up_weight, inputs_full)
    hidden = (silu_parts(gate_val)[0] * up_val).astype(jnp.bfloat16)
    hidden_pair = jnp.concatenate([hidden, lax.ppermute(hidden, "dp", SIBLING)], axis=1)

    down_part = pl.pallas_call(
        down_kernel,
        out_shape=jax.ShapeDtypeStruct((8, 2 * tokens, width), jnp.float32),
        in_specs=[smem, vmem, vmem],
        out_specs=vmem,
        compiler_params=pltpu.CompilerParams(vmem_limit_bytes=16 * 2**20),
        cost_estimate=pl.CostEstimate(
            flops=2 * 256 * 448 * 2048, bytes_accessed=6 * 2**20, transcendentals=0
        ),
    )(where, hidden_pair, down_weight)
    projected = jnp.einsum(
        "tk,zkn->ztn",
        teacher_pair,
        projector_line,
        preferred_element_type=jnp.float32,
    )
    part = (down_part - projected * scale_pair).astype(jnp.bfloat16)
    mine, other = part[:, :tokens], part[:, tokens:]
    other = lax.ppermute(other, "dp", SIBLING)
    parts = jnp.stack(
        [jnp.where(core == 0, mine, other), jnp.where(core == 0, other, mine)], axis=1
    ).reshape(16, tokens, width)
    gates = jnp.concatenate([gate_val, up_val], axis=0)
    gates, parts, inputs_swapped = lax.optimization_barrier((gates, parts, inputs_swapped))
    gates_line = lax.all_gather(gates, "dp", axis=0, axis_index_groups=LINES)
    mismatch = student_input.astype(jnp.float32) + scatter_sum(parts)

    row_loss = jnp.sum(mismatch * mismatch, axis=1)
    outgrad_part = (mismatch / tokens_all).astype(jnp.bfloat16)
    outgrad_gathered = gather_group(with_rows(outgrad_part, row_loss))
    outgrad_moved = lax.ppermute(outgrad_part, EVERY, SWAP)

    grad_hidden = pl.pallas_call(
        functools.partial(hidden_kernel, tokens),
        out_shape=jax.ShapeDtypeStruct((units + 32, tokens), jnp.bfloat16),
        in_specs=[vmem, vmem],
        out_specs=vmem,
        compiler_params=pltpu.CompilerParams(vmem_limit_bytes=16 * 2**20),
        cost_estimate=pl.CostEstimate(
            flops=2 * 128 * 448 * 4096, bytes_accessed=5 * 2**20, transcendentals=0
        ),
    )(outgrad_gathered, down_weight)
    outgrad_moved, _ = lax.optimization_barrier((outgrad_moved, grad_hidden))
    outgrad_swapped = gather_group(outgrad_moved)
    line = ring(grad_hidden)
    line_loss = jnp.stack([found[-1][1][units - found[-1][0] :] for found in line])
    line_loss = rows_of(line_loss, 0, tokens)
    spans = [[(first, min(piece.shape[0], units - first)) for first, piece in found] for found in line]
    pieces = [piece for found in line for _, piece in found]

    grad = jax.ShapeDtypeStruct((units, width), jnp.float32)
    *theirs, mine = pl.pallas_call(
        functools.partial(grads_kernel, tokens, spans),
        out_shape=(grad, grad, grad, jax.ShapeDtypeStruct((3, units, width), jnp.float32)),
        in_specs=[smem] + [anywhere] * (3 + len(pieces)),
        out_specs=(vmem,) * 4,
        scratch_shapes=[
            pltpu.VMEM(gates_line.shape, jnp.float32),
            pltpu.VMEM(inputs_swapped.shape, jnp.bfloat16),
            pltpu.VMEM(outgrad_swapped.shape, jnp.bfloat16),
            pltpu.VMEM((8, units, tokens), jnp.bfloat16),
            pltpu.VMEM((3, units, 8 * tokens), jnp.bfloat16),
            pltpu.SemaphoreType.DMA((10 + len(pieces),)),
        ],
        compiler_params=pltpu.CompilerParams(vmem_limit_bytes=60 * 2**20),
        cost_estimate=pl.CostEstimate(
            flops=2 * 3 * 1024 * 448 * 512, bytes_accessed=10 * 2**20, transcendentals=2**19
        ),
    )(where, gates_line, inputs_swapped, outgrad_swapped, *pieces)
    theirs = [lax.ppermute(part, "dp", SIBLING) for part in theirs]
    grad_gate, grad_up, grad_down = [mine[part] + theirs[part] for part in range(3)]
    all_loss = line_loss + lax.ppermute(line_loss, "dp", SIBLING)
    loss_value = 0.5 * jnp.sum(all_loss) / tokens_all
    return (loss_value, grad_gate, grad_up, grad_down)


def solution(mesh):
    in_specs = (
        P("dp", ("sec", "tp")),
        P("dp", ("sec", "tp")),
        P(("sec", "tp"), "dp"),
        P(("sec", "tp"), None),
        P(("sec", "tp"), None),
        P(("sec", "tp"), None),
    )
    out_specs = (P(), P(("sec", "tp"), "dp"), P(("sec", "tp"), "dp"), P(("sec", "tp"), "dp"))
    return jax.shard_map(shards, mesh=mesh, in_specs=in_specs, out_specs=out_specs, check_vma=False)
```

```python
import functools

import jax
import jax.numpy as jnp
from jax import lax
from jax.experimental import pallas as pl
from jax.experimental.pallas import tpu as pltpu
from jax.sharding import PartitionSpec as P

epsilon = 1e-05

GROUP = ("sec", "tp")
EVERY = ("sec", "tp", "dp")
LINES = [[2 * z + c for z in range(8)] for c in range(2)]
SIBLING = [(d, d ^ 1) for d in range(16)]
SWAP = [
    (s * 16 + d, ((d & 14) | (s & 1)) * 16 + ((s & 14) | (d & 1)))
    for s in range(16)
    for d in range(16)
]


def silu_parts(gate_val):
    sigma = jax.nn.sigmoid(gate_val)
    return (gate_val * sigma, sigma * (1.0 + gate_val * (1.0 - sigma)))


def contract_cols(left, right):
    return lax.dot_general(
        left, right, (((1,), (1,)), ((), ())), preferred_element_type=jnp.float32
    )


def gather_group(block):
    copies = jnp.broadcast_to(block[None], (16,) + block.shape)
    return lax.all_to_all(copies, GROUP, 0, 0, tiled=True)


RIGHT = [(d, (d + 2) % 16) for d in range(16)]
LEFT = [(d, (d - 2) % 16) for d in range(16)]


def ring(block):
    half = block.shape[0] // 2
    up = down = block
    found = [[(0, block)]] + [[] for _ in range(7)]
    for step in range(1, 4):
        up, down = lax.ppermute(up, "dp", RIGHT), lax.ppermute(down, "dp", LEFT)
        found[-step], found[step] = [(0, up)], [(0, down)]
    up, down = lax.ppermute(up[:half], "dp", RIGHT), lax.ppermute(down[half:], "dp", LEFT)
    found[4] = [(0, up), (half, down)]
    return found


def fetch(pairs, sems):
    copies = [pltpu.make_async_copy(src, dst, sems.at[i]) for i, (src, dst) in enumerate(pairs)]
    for copy in copies:
        copy.start()
    return copies


def down_kernel(place_ref, hidden_ref, down_ref, out_ref):
    width = out_ref.shape[2]
    for i in range(8):
        columns = pl.ds(pl.multiple_of((2 * i + place_ref[1]) * width, width), width)
        out_ref[i] = lax.dot_general(
            hidden_ref[...],
            down_ref[:, columns],
            (((0,), (0,)), ((), ())),
            preferred_element_type=jnp.float32,
        )


def split_rows(value, count):
    high = value.astype(jnp.bfloat16).astype(jnp.float32)
    mid = (value - high).astype(jnp.bfloat16).astype(jnp.float32)
    shape = (count, value.shape[1])
    row = lax.broadcasted_iota(jnp.int32, shape, 0)
    rows = jnp.zeros(shape, jnp.float32)
    for i, part in enumerate((high, mid, value - high - mid)):
        rows = jnp.where(row == i, jnp.broadcast_to(part, shape), rows)
    return rows.astype(jnp.bfloat16)


def mismatch_kernel(tokens_all, blocks_ref, inputs_ref, copies_ref, outgrad_ref):
    tokens = inputs_ref.shape[0]
    mismatch = blocks_ref[0].astype(jnp.float32)
    for i in range(1, 16):
        mismatch = mismatch + blocks_ref[i].astype(jnp.float32)
    mismatch = inputs_ref[...].astype(jnp.float32) + mismatch
    loss = jnp.sum(mismatch * mismatch, axis=0, keepdims=True)
    loss = split_rows(loss[:, :tokens] + loss[:, tokens:], 16)
    loss = jnp.concatenate([loss, jnp.zeros_like(loss)], axis=1)
    outgrad = (mismatch * (1.0 / tokens_all)).astype(jnp.bfloat16)
    outgrad_ref[...] = outgrad
    for i in range(16):
        copies_ref[i, :tokens] = outgrad
        copies_ref[i, tokens:] = loss


def hidden_kernel(tokens, blocks_ref, down_ref, out_ref):
    width = blocks_ref.shape[2]
    units = down_ref.shape[0]
    total = loss = None
    for i in range(16):
        found = contract_cols(down_ref[:, i * width : (i + 1) * width], blocks_ref[i, :tokens])
        total = found if total is None else total + found
        rows = blocks_ref[i, tokens : tokens + 16, :tokens].astype(jnp.float32)
        loss = rows if loss is None else loss + rows
    out_ref[:units] = total.astype(out_ref.dtype)
    loss = jnp.sum(loss, axis=0, keepdims=True)
    out_ref[units:] = split_rows(loss, out_ref.shape[0] - units)


def columns_of(ref, half, start):
    return jnp.concatenate(
        [ref[2 * lax.rem(start + i, 8) + half] for i in range(8)], axis=0
    )


def grads_kernel(tokens, spans, place_ref, gates_hbm, inputs_hbm, outgrads_hbm, *refs):
    count = sum(len(span) for span in spans)
    blocks, theirs_refs, mine_ref = refs[:count], refs[count : count + 3], refs[count + 3]
    gates_ref, inputs_ref, outgrads_ref, block_ref, lefts_ref, sems = refs[count + 4 :]
    start, core = place_ref[0], place_ref[1]
    units = lefts_ref.shape[1]
    spots = [lax.rem(start + i, 8) for i in range(8)]
    pieces = iter(blocks)
    pairs = []
    for i, span in enumerate(spans):
        pairs.append((gates_hbm.at[spots[i]], gates_ref.at[i]))
        for first, rows in span:
            source = next(pieces).at[pl.ds(0, rows)]
            pairs.append((source, block_ref.at[i, pl.ds(first, rows)]))
    pairs += [(inputs_hbm, inputs_ref), (outgrads_hbm, outgrads_ref)]
    waiting = iter(fetch(pairs, sems))
    for i in range(8):
        for _ in range(1 + len(spans[i])):
            next(waiting).wait()
        columns = pl.ds(i * tokens, tokens)
        gate, up = gates_ref[i, :units], gates_ref[i, units:]
        grad_hidden = block_ref[i].astype(jnp.float32)
        activated, slope = silu_parts(gate)
        lefts_ref[0, :, columns] = (grad_hidden * up * slope).astype(jnp.bfloat16)
        lefts_ref[1, :, columns] = (grad_hidden * activated).astype(jnp.bfloat16)
        lefts_ref[2, :, columns] = (activated * up).astype(jnp.bfloat16)
    for copy in waiting:
        copy.wait()
    for mine, half in ((False, 1 - core), (True, core)):
        inputs = columns_of(inputs_ref, half, start)
        outgrads = columns_of(outgrads_ref, half, start)
        for part, right in enumerate((inputs, inputs, outgrads)):
            found = jnp.dot(lefts_ref[part], right, preferred_element_type=jnp.float32)
            if mine:
                mine_ref[part] = found
            else:
                theirs_refs[part][...] = found


def scatter_sum(parts):
    return jnp.sum(
        lax.all_to_all(parts, GROUP, 0, 0, tiled=True).astype(jnp.float32), axis=0
    )


def split3(value):
    high = lax.reduce_precision(value, 8, 7)
    mid = lax.reduce_precision(value - high, 8, 7)
    low = value - high - mid
    return jnp.stack([high, mid, low]).astype(jnp.bfloat16)


def with_rows(block, extra):
    columns = block.shape[1]
    rows = jnp.pad(split3(extra), ((0, 13), (0, columns - extra.shape[0])))
    return jnp.concatenate([block, rows], axis=0)


def rows_of(blocks, tokens, count):
    rows = blocks[:, tokens : tokens + 3, :count].astype(jnp.float32)
    return jnp.sum(jnp.sum(rows, axis=1), axis=0)


def shards(student_input, teacher_hidden, projector, gate_weight, up_weight, down_weight):
    tokens, width = student_input.shape
    units = gate_weight.shape[0]
    tokens_all = tokens * 16
    teacher_units = teacher_hidden.shape[1] * 16
    place = lax.axis_index("dp")
    core = lax.rem(place, 2)
    start = lax.div(place, 2)
    where = jnp.stack([start, core])
    vmem, anywhere = pl.BlockSpec(memory_space=pltpu.VMEM), pl.BlockSpec(memory_space=pl.ANY)
    smem = pl.BlockSpec(memory_space=pltpu.SMEM)

    projector_line = lax.all_gather(projector, "dp", axis=0, axis_index_groups=LINES)
    inputs_moved = lax.ppermute(student_input, EVERY, SWAP)
    teacher_pair = jnp.concatenate(
        [teacher_hidden, lax.ppermute(teacher_hidden, "dp", SIBLING)], axis=0
    )
    teacher_float = teacher_hidden.astype(jnp.float32)
    squares = jnp.sum(teacher_float * teacher_float, axis=1)

    gathered = gather_group(with_rows(student_input, squares))
    inputs_moved, _ = lax.optimization_barrier((inputs_moved, gathered))
    inputs_swapped = gather_group(inputs_moved)
    row_total = rows_of(gathered, tokens, tokens)
    row_scale = 1.0 / jnp.sqrt(row_total / teacher_units + epsilon)
    scale_pair = jnp.concatenate([row_scale, lax.ppermute(row_scale, "dp", SIBLING)])[:, None]
    inputs_full = gathered[:, :tokens].transpose(1, 0, 2).reshape(tokens, 16 * width)

    gate_val = contract_cols(gate_weight, inputs_full)
    up_val = contract_cols(up_weight, inputs_full)
    hidden = (silu_parts(gate_val)[0] * up_val).astype(jnp.bfloat16)
    hidden_pair = jnp.concatenate([hidden, lax.ppermute(hidden, "dp", SIBLING)], axis=1)

    down_part = pl.pallas_call(
        down_kernel,
        out_shape=jax.ShapeDtypeStruct((8, 2 * tokens, width), jnp.float32),
        in_specs=[smem, vmem, vmem],
        out_specs=vmem,
        compiler_params=pltpu.CompilerParams(vmem_limit_bytes=16 * 2**20),
        cost_estimate=pl.CostEstimate(
            flops=2 * 256 * 448 * 2048, bytes_accessed=6 * 2**20, transcendentals=0
        ),
    )(where, hidden_pair, down_weight)
    projected = jnp.einsum(
        "tk,zkn->ztn",
        teacher_pair,
        projector_line,
        preferred_element_type=jnp.float32,
    )
    part = (down_part - projected * scale_pair).astype(jnp.bfloat16)
    mine, other = part[:, :tokens], part[:, tokens:]
    other = lax.ppermute(other, "dp", SIBLING)
    parts = jnp.stack(
        [jnp.where(core == 0, mine, other), jnp.where(core == 0, other, mine)], axis=1
    ).reshape(16, tokens, width)
    gates = jnp.concatenate([gate_val, up_val], axis=0)
    gates, parts, inputs_swapped = lax.optimization_barrier((gates, parts, inputs_swapped))
    gates_line = lax.all_gather(gates, "dp", axis=0, axis_index_groups=LINES)
    blocks = lax.all_to_all(parts, GROUP, 0, 0, tiled=True)
    copies, outgrad_part = pl.pallas_call(
        functools.partial(mismatch_kernel, tokens_all),
        out_shape=(
            jax.ShapeDtypeStruct((16, tokens + 16, width), jnp.bfloat16),
            jax.ShapeDtypeStruct((tokens, width), jnp.bfloat16),
        ),
        in_specs=[vmem, vmem],
        out_specs=(vmem, vmem),
        compiler_params=pltpu.CompilerParams(vmem_limit_bytes=16 * 2**20),
        cost_estimate=pl.CostEstimate(
            flops=2**20, bytes_accessed=3 * 2**20, transcendentals=0
        ),
    )(blocks, student_input)
    outgrad_gathered = lax.all_to_all(copies, GROUP, 0, 0, tiled=True)
    outgrad_moved = lax.ppermute(outgrad_part, EVERY, SWAP)

    grad_hidden = pl.pallas_call(
        functools.partial(hidden_kernel, tokens),
        out_shape=jax.ShapeDtypeStruct((units + 32, tokens), jnp.bfloat16),
        in_specs=[vmem, vmem],
        out_specs=vmem,
        compiler_params=pltpu.CompilerParams(vmem_limit_bytes=16 * 2**20),
        cost_estimate=pl.CostEstimate(
            flops=2 * 128 * 448 * 4096, bytes_accessed=5 * 2**20, transcendentals=0
        ),
    )(outgrad_gathered, down_weight)
    outgrad_moved, _ = lax.optimization_barrier((outgrad_moved, grad_hidden))
    outgrad_swapped = gather_group(outgrad_moved)
    line = ring(grad_hidden)
    line_loss = jnp.stack([found[-1][1][units - found[-1][0] :] for found in line])
    line_loss = rows_of(line_loss, 0, tokens)
    spans = [[(first, min(piece.shape[0], units - first)) for first, piece in found] for found in line]
    pieces = [piece for found in line for _, piece in found]

    grad = jax.ShapeDtypeStruct((units, width), jnp.float32)
    *theirs, mine = pl.pallas_call(
        functools.partial(grads_kernel, tokens, spans),
        out_shape=(grad, grad, grad, jax.ShapeDtypeStruct((3, units, width), jnp.float32)),
        in_specs=[smem] + [anywhere] * (3 + len(pieces)),
        out_specs=(vmem,) * 4,
        scratch_shapes=[
            pltpu.VMEM(gates_line.shape, jnp.float32),
            pltpu.VMEM(inputs_swapped.shape, jnp.bfloat16),
            pltpu.VMEM(outgrad_swapped.shape, jnp.bfloat16),
            pltpu.VMEM((8, units, tokens), jnp.bfloat16),
            pltpu.VMEM((3, units, 8 * tokens), jnp.bfloat16),
            pltpu.SemaphoreType.DMA((10 + len(pieces),)),
        ],
        compiler_params=pltpu.CompilerParams(vmem_limit_bytes=60 * 2**20),
        cost_estimate=pl.CostEstimate(
            flops=2 * 3 * 1024 * 448 * 512, bytes_accessed=10 * 2**20, transcendentals=2**19
        ),
    )(where, gates_line, inputs_swapped, outgrad_swapped, *pieces)
    theirs = [lax.ppermute(part, "dp", SIBLING) for part in theirs]
    grad_gate, grad_up, grad_down = [mine[part] + theirs[part] for part in range(3)]
    all_loss = line_loss + lax.ppermute(line_loss, "dp", SIBLING)
    loss_value = 0.5 * jnp.sum(all_loss) / tokens_all
    return (loss_value, grad_gate, grad_up, grad_down)


def solution(mesh):
    in_specs = (
        P("dp", ("sec", "tp")),
        P("dp", ("sec", "tp")),
        P(("sec", "tp"), "dp"),
        P(("sec", "tp"), None),
        P(("sec", "tp"), None),
        P(("sec", "tp"), None),
    )
    out_specs = (P(), P(("sec", "tp"), "dp"), P(("sec", "tp"), "dp"), P(("sec", "tp"), "dp"))
    return jax.shard_map(shards, mesh=mesh, in_specs=in_specs, out_specs=out_specs, check_vma=False)
```

```python
import functools

import jax
import jax.numpy as jnp
from jax import lax
from jax.experimental import pallas as pl
from jax.experimental.pallas import tpu as pltpu
from jax.sharding import PartitionSpec as P

epsilon = 1e-05

GROUP = ("sec", "tp")
EVERY = ("sec", "tp", "dp")
LINES = [[2 * z + c for z in range(8)] for c in range(2)]
SIBLING = [(d, d ^ 1) for d in range(16)]
SWAP = [
    (s * 16 + d, ((d & 14) | (s & 1)) * 16 + ((s & 14) | (d & 1)))
    for s in range(16)
    for d in range(16)
]


def silu_parts(gate_val):
    sigma = jax.nn.sigmoid(gate_val)
    return (gate_val * sigma, sigma * (1.0 + gate_val * (1.0 - sigma)))


def contract_cols(left, right):
    return lax.dot_general(
        left, right, (((1,), (1,)), ((), ())), preferred_element_type=jnp.float32
    )


def gather_group(block):
    copies = jnp.broadcast_to(block[None], (16,) + block.shape)
    return lax.all_to_all(copies, GROUP, 0, 0, tiled=True)


RIGHT = [(d, (d + 2) % 16) for d in range(16)]
LEFT = [(d, (d - 2) % 16) for d in range(16)]


def ring(block):
    half = block.shape[0] // 2
    up = down = block
    found = [[(0, block)]] + [[] for _ in range(7)]
    for step in range(1, 4):
        up, down = lax.ppermute(up, "dp", RIGHT), lax.ppermute(down, "dp", LEFT)
        found[-step], found[step] = [(0, up)], [(0, down)]
    up, down = lax.ppermute(up[:half], "dp", RIGHT), lax.ppermute(down[half:], "dp", LEFT)
    found[4] = [(0, up), (half, down)]
    return found


def fetch(pairs, sems):
    copies = [pltpu.make_async_copy(src, dst, sems.at[i]) for i, (src, dst) in enumerate(pairs)]
    for copy in copies:
        copy.start()
    return copies


def down_kernel(place_ref, hidden_ref, down_ref, out_ref):
    width = out_ref.shape[2]
    for i in range(8):
        columns = pl.ds(pl.multiple_of((2 * i + place_ref[1]) * width, width), width)
        out_ref[i] = lax.dot_general(
            hidden_ref[...],
            down_ref[:, columns],
            (((0,), (0,)), ((), ())),
            preferred_element_type=jnp.float32,
        )


def split_rows(value, count):
    high = value.astype(jnp.bfloat16).astype(jnp.float32)
    mid = (value - high).astype(jnp.bfloat16).astype(jnp.float32)
    shape = (count, value.shape[1])
    row = lax.broadcasted_iota(jnp.int32, shape, 0)
    rows = jnp.zeros(shape, jnp.float32)
    for i, part in enumerate((high, mid, value - high - mid)):
        rows = jnp.where(row == i, jnp.broadcast_to(part, shape), rows)
    return rows.astype(jnp.bfloat16)


def mismatch_kernel(tokens_all, blocks_ref, inputs_ref, copies_ref, outgrad_ref):
    tokens = inputs_ref.shape[0]
    mismatch = blocks_ref[0].astype(jnp.float32)
    for i in range(1, 16):
        mismatch = mismatch + blocks_ref[i].astype(jnp.float32)
    mismatch = inputs_ref[...].astype(jnp.float32) + mismatch
    loss = jnp.sum(mismatch * mismatch, axis=0, keepdims=True)
    loss = split_rows(loss[:, :tokens] + loss[:, tokens:], 16)
    loss = jnp.concatenate([loss, jnp.zeros_like(loss)], axis=1)
    outgrad = (mismatch * (1.0 / tokens_all)).astype(jnp.bfloat16)
    outgrad_ref[...] = outgrad
    for i in range(16):
        copies_ref[i, :tokens] = outgrad
        copies_ref[i, tokens:] = loss


def copies_kernel(block_ref, copies_ref):
    for i in range(copies_ref.shape[0]):
        copies_ref[i] = block_ref[...]


def hidden_kernel(tokens, blocks_ref, down_ref, out_ref):
    width = blocks_ref.shape[2]
    units = down_ref.shape[0]
    total = loss = None
    for i in range(16):
        found = contract_cols(down_ref[:, i * width : (i + 1) * width], blocks_ref[i, :tokens])
        total = found if total is None else total + found
        rows = blocks_ref[i, tokens : tokens + 16, :tokens].astype(jnp.float32)
        loss = rows if loss is None else loss + rows
    out_ref[:units] = total.astype(out_ref.dtype)
    loss = jnp.sum(loss, axis=0, keepdims=True)
    out_ref[units:] = split_rows(loss, out_ref.shape[0] - units)


def columns_of(ref, half, start):
    return jnp.concatenate(
        [ref[2 * lax.rem(start + i, 8) + half] for i in range(8)], axis=0
    )


def grads_kernel(tokens, spans, place_ref, gates_hbm, inputs_hbm, outgrads_hbm, *refs):
    count = sum(len(span) for span in spans)
    blocks, theirs_refs, mine_ref = refs[:count], refs[count : count + 3], refs[count + 3]
    gates_ref, inputs_ref, outgrads_ref, block_ref, lefts_ref, sems = refs[count + 4 :]
    start, core = place_ref[0], place_ref[1]
    units = lefts_ref.shape[1]
    spots = [lax.rem(start + i, 8) for i in range(8)]
    pieces = iter(blocks)
    pairs = []
    for i, span in enumerate(spans):
        pairs.append((gates_hbm.at[spots[i]], gates_ref.at[i]))
        for first, rows in span:
            source = next(pieces).at[pl.ds(0, rows)]
            pairs.append((source, block_ref.at[i, pl.ds(first, rows)]))
    pairs += [(inputs_hbm, inputs_ref), (outgrads_hbm, outgrads_ref)]
    waiting = iter(fetch(pairs, sems))
    for i in range(8):
        for _ in range(1 + len(spans[i])):
            next(waiting).wait()
        columns = pl.ds(i * tokens, tokens)
        gate, up = gates_ref[i, :units], gates_ref[i, units:]
        grad_hidden = block_ref[i].astype(jnp.float32)
        activated, slope = silu_parts(gate)
        lefts_ref[0, :, columns] = (grad_hidden * up * slope).astype(jnp.bfloat16)
        lefts_ref[1, :, columns] = (grad_hidden * activated).astype(jnp.bfloat16)
        lefts_ref[2, :, columns] = (activated * up).astype(jnp.bfloat16)
    for copy in waiting:
        copy.wait()
    for mine, half in ((False, 1 - core), (True, core)):
        inputs = columns_of(inputs_ref, half, start)
        outgrads = columns_of(outgrads_ref, half, start)
        for part, right in enumerate((inputs, inputs, outgrads)):
            found = jnp.dot(lefts_ref[part], right, preferred_element_type=jnp.float32)
            if mine:
                mine_ref[part] = found
            else:
                theirs_refs[part][...] = found


def scatter_sum(parts):
    return jnp.sum(
        lax.all_to_all(parts, GROUP, 0, 0, tiled=True).astype(jnp.float32), axis=0
    )


def split3(value):
    high = lax.reduce_precision(value, 8, 7)
    mid = lax.reduce_precision(value - high, 8, 7)
    low = value - high - mid
    return jnp.stack([high, mid, low]).astype(jnp.bfloat16)


def with_rows(block, extra):
    columns = block.shape[1]
    rows = jnp.pad(split3(extra), ((0, 13), (0, columns - extra.shape[0])))
    return jnp.concatenate([block, rows], axis=0)


def rows_of(blocks, tokens, count):
    rows = blocks[:, tokens : tokens + 3, :count].astype(jnp.float32)
    return jnp.sum(jnp.sum(rows, axis=1), axis=0)


def shards(student_input, teacher_hidden, projector, gate_weight, up_weight, down_weight):
    tokens, width = student_input.shape
    units = gate_weight.shape[0]
    tokens_all = tokens * 16
    teacher_units = teacher_hidden.shape[1] * 16
    place = lax.axis_index("dp")
    core = lax.rem(place, 2)
    start = lax.div(place, 2)
    where = jnp.stack([start, core])
    vmem, anywhere = pl.BlockSpec(memory_space=pltpu.VMEM), pl.BlockSpec(memory_space=pl.ANY)
    smem = pl.BlockSpec(memory_space=pltpu.SMEM)

    projector_line = lax.all_gather(projector, "dp", axis=0, axis_index_groups=LINES)
    inputs_moved = lax.ppermute(student_input, EVERY, SWAP)
    teacher_pair = jnp.concatenate(
        [teacher_hidden, lax.ppermute(teacher_hidden, "dp", SIBLING)], axis=0
    )
    teacher_float = teacher_hidden.astype(jnp.float32)
    squares = jnp.sum(teacher_float * teacher_float, axis=1)

    gathered = gather_group(with_rows(student_input, squares))
    inputs_moved, _ = lax.optimization_barrier((inputs_moved, gathered))
    inputs_swapped = gather_group(inputs_moved)
    row_total = rows_of(gathered, tokens, tokens)
    row_scale = 1.0 / jnp.sqrt(row_total / teacher_units + epsilon)
    scale_pair = jnp.concatenate([row_scale, lax.ppermute(row_scale, "dp", SIBLING)])[:, None]
    inputs_full = gathered[:, :tokens].transpose(1, 0, 2).reshape(tokens, 16 * width)

    gate_val = contract_cols(gate_weight, inputs_full)
    up_val = contract_cols(up_weight, inputs_full)
    hidden = (silu_parts(gate_val)[0] * up_val).astype(jnp.bfloat16)
    hidden_pair = jnp.concatenate([hidden, lax.ppermute(hidden, "dp", SIBLING)], axis=1)

    down_part = pl.pallas_call(
        down_kernel,
        out_shape=jax.ShapeDtypeStruct((8, 2 * tokens, width), jnp.float32),
        in_specs=[smem, vmem, vmem],
        out_specs=vmem,
        compiler_params=pltpu.CompilerParams(vmem_limit_bytes=16 * 2**20),
        cost_estimate=pl.CostEstimate(
            flops=2 * 256 * 448 * 2048, bytes_accessed=6 * 2**20, transcendentals=0
        ),
    )(where, hidden_pair, down_weight)
    projected = jnp.einsum(
        "tk,zkn->ztn",
        teacher_pair,
        projector_line,
        preferred_element_type=jnp.float32,
    )
    part = (down_part - projected * scale_pair).astype(jnp.bfloat16)
    mine, other = part[:, :tokens], part[:, tokens:]
    other = lax.ppermute(other, "dp", SIBLING)
    parts = jnp.stack(
        [jnp.where(core == 0, mine, other), jnp.where(core == 0, other, mine)], axis=1
    ).reshape(16, tokens, width)
    gates = jnp.concatenate([gate_val, up_val], axis=0)
    gates, parts, inputs_swapped = lax.optimization_barrier((gates, parts, inputs_swapped))
    gates_line = lax.all_gather(gates, "dp", axis=0, axis_index_groups=LINES)
    blocks = lax.all_to_all(parts, GROUP, 0, 0, tiled=True)
    copies, outgrad_part = pl.pallas_call(
        functools.partial(mismatch_kernel, tokens_all),
        out_shape=(
            jax.ShapeDtypeStruct((16, tokens + 16, width), jnp.bfloat16),
            jax.ShapeDtypeStruct((tokens, width), jnp.bfloat16),
        ),
        in_specs=[vmem, vmem],
        out_specs=(vmem, vmem),
        compiler_params=pltpu.CompilerParams(vmem_limit_bytes=16 * 2**20),
        cost_estimate=pl.CostEstimate(
            flops=2**20, bytes_accessed=3 * 2**20, transcendentals=0
        ),
    )(blocks, student_input)
    outgrad_gathered = lax.all_to_all(copies, GROUP, 0, 0, tiled=True)
    outgrad_moved = lax.ppermute(outgrad_part, EVERY, SWAP)

    grad_hidden = pl.pallas_call(
        functools.partial(hidden_kernel, tokens),
        out_shape=jax.ShapeDtypeStruct((units + 32, tokens), jnp.bfloat16),
        in_specs=[vmem, vmem],
        out_specs=vmem,
        compiler_params=pltpu.CompilerParams(vmem_limit_bytes=16 * 2**20),
        cost_estimate=pl.CostEstimate(
            flops=2 * 128 * 448 * 4096, bytes_accessed=5 * 2**20, transcendentals=0
        ),
    )(outgrad_gathered, down_weight)
    moved_copies = pl.pallas_call(
        copies_kernel,
        out_shape=jax.ShapeDtypeStruct((16, tokens, width), jnp.bfloat16),
        in_specs=[vmem],
        out_specs=vmem,
        compiler_params=pltpu.CompilerParams(vmem_limit_bytes=16 * 2**20),
        cost_estimate=pl.CostEstimate(flops=0, bytes_accessed=2 * 2**20, transcendentals=0),
    )(outgrad_moved)
    moved_copies, _ = lax.optimization_barrier((moved_copies, grad_hidden))
    outgrad_swapped = lax.all_to_all(moved_copies, GROUP, 0, 0, tiled=True)
    line = ring(grad_hidden)
    line_loss = jnp.stack([found[-1][1][units - found[-1][0] :] for found in line])
    line_loss = rows_of(line_loss, 0, tokens)
    spans = [[(first, min(piece.shape[0], units - first)) for first, piece in found] for found in line]
    pieces = [piece for found in line for _, piece in found]

    grad = jax.ShapeDtypeStruct((units, width), jnp.float32)
    *theirs, mine = pl.pallas_call(
        functools.partial(grads_kernel, tokens, spans),
        out_shape=(grad, grad, grad, jax.ShapeDtypeStruct((3, units, width), jnp.float32)),
        in_specs=[smem] + [anywhere] * (3 + len(pieces)),
        out_specs=(vmem,) * 4,
        scratch_shapes=[
            pltpu.VMEM(gates_line.shape, jnp.float32),
            pltpu.VMEM(inputs_swapped.shape, jnp.bfloat16),
            pltpu.VMEM(outgrad_swapped.shape, jnp.bfloat16),
            pltpu.VMEM((8, units, tokens), jnp.bfloat16),
            pltpu.VMEM((3, units, 8 * tokens), jnp.bfloat16),
            pltpu.SemaphoreType.DMA((10 + len(pieces),)),
        ],
        compiler_params=pltpu.CompilerParams(vmem_limit_bytes=60 * 2**20),
        cost_estimate=pl.CostEstimate(
            flops=2 * 3 * 1024 * 448 * 512, bytes_accessed=10 * 2**20, transcendentals=2**19
        ),
    )(where, gates_line, inputs_swapped, outgrad_swapped, *pieces)
    theirs = [lax.ppermute(part, "dp", SIBLING) for part in theirs]
    grad_gate, grad_up, grad_down = [mine[part] + theirs[part] for part in range(3)]
    all_loss = line_loss + lax.ppermute(line_loss, "dp", SIBLING)
    loss_value = 0.5 * jnp.sum(all_loss) / tokens_all
    return (loss_value, grad_gate, grad_up, grad_down)


def solution(mesh):
    in_specs = (
        P("dp", ("sec", "tp")),
        P("dp", ("sec", "tp")),
        P(("sec", "tp"), "dp"),
        P(("sec", "tp"), None),
        P(("sec", "tp"), None),
        P(("sec", "tp"), None),
    )
    out_specs = (P(), P(("sec", "tp"), "dp"), P(("sec", "tp"), "dp"), P(("sec", "tp"), "dp"))
    return jax.shard_map(shards, mesh=mesh, in_specs=in_specs, out_specs=out_specs, check_vma=False)
```
